32 devices in a mesh: wide: 8 (over z, y), narrow: 4 (over x, core).
Axes of the slice: x: 2, y: 2, z: 4, core: 2. Of those that a mesh axis runs over, the one named last changes fastest.
Arguments:
- queries: bfloat16 [16, 128, 2304], P('wide'), may hold values from -112 to 112
- new_kv: bfloat16 [16, 2, 128, 2304], P('wide', None, 'narrow'), may hold values from -4 to 4
- cache_pool: bfloat16 [16, 16, 2, 128, 2304], P('wide', 'narrow'), may hold values from -4 to 4
- page_table: int32 [16, 16], P('wide'), may hold values from 0 to 15, as said below
- cached_len: int32 [16], P('wide'), may hold values from 0 to 2048, as said below
- residual: bfloat16 [2048, 2304], P('wide'), may hold values from -0.1796875 to 0.1796875
- norm_gain: float32 [2304], replicated, may hold values from 0.1 to 1.9
- expert_ids: int32 [2048, 2], P('wide'), may hold values from 0 to 7, all different within a row; in each aligned block of 256 rows (0 to 255, 256 to 511, ...) at most 80 rows name the same one
- route_weight: float32 [2048, 2], P('wide'), may hold values from 0.1 to 1
- w_gate_up: bfloat16 [8, 2304, 2, 5760], P(None, 'narrow', None, 'wide'), may hold values from -0.125 to 0.125
- w_down: bfloat16 [8, 5760, 2304], P(None, 'wide', 'narrow'), may hold values from -0.078125 to 0.078125
Outputs:
- layer_out: bfloat16 [2048, 2304], P('wide', 'narrow')
The draws below stay inside these ranges and needn't reach their ends.
Inputs may be any that keep to these rules, and one draw needn't show every extreme that they name: `page_table`: for each request the 16 entries are distinct, and entry j lies in (j % 4) * 4 to (j % 4) * 4 + 3. `cached_len`: some request has exactly 2048 cached tokens. `expert_ids`: A token's two experts differ; among the 256 tokens of one index of wide no expert is named more than 80 times.
All inputs are finite; a program needn't handle non-finite values.
Results may differ from the reference program's by a relative error of at most 0.035.
Values may be sent and summed in bfloat16 or wider, within the bound.
A program may use at most 192 MiB of HBM per device.

```python
import math
import jax
import jax.numpy as jnp
import numpy as np
from jax import lax

D = 2304
HEADS = 36
HD = 64
FF = 5760
E = 8
NEWTOK = 128
PAGE = 128
PG_DEV = 4
REQS = 16
TOKENS = 2048
TOKW = 256
MAXPG = 16
CAP = 80
N_WIDE = 8
N_NARROW = 4


def joint_draw(key):
    folded = jax.random.fold_in(key, 29)
    query_key, pair_key = jax.random.split(folded)
    queries = jnp.clip(jax.random.normal(query_key, (REQS, NEWTOK, D), jnp.float32), -4.0, 4.0)
    new_kv = jnp.clip(jax.random.normal(pair_key, (REQS, 2, NEWTOK, D), jnp.float32), -4.0, 4.0)
    return (queries, new_kv)


def draw_queries(key, part):
    return joint_draw(key)[0].astype(jnp.bfloat16)


def draw_new_kv(key, part):
    return joint_draw(key)[1].astype(jnp.bfloat16)


def draw_page_table(key, part):
    groups = MAXPG // PG_DEV
    scores = jax.random.randint(jax.random.fold_in(key, 31), (REQS, groups, PG_DEV), 0, 1 << 20)
    distinct = scores * PG_DEV + jnp.arange(PG_DEV, dtype=jnp.int32)[None, None, :]
    ranking = jnp.argsort(distinct, axis=2).astype(jnp.int32)
    slot_ids = jnp.arange(groups, dtype=jnp.int32)[None, :, None] * PG_DEV + ranking
    return jnp.transpose(slot_ids, (0, 2, 1)).reshape(REQS, MAXPG)


def draw_cached_len(key, part):
    longest = PAGE * MAXPG
    first_key, second_key = jax.random.split(jax.random.fold_in(key, 37))
    attempts = jax.random.randint(first_key, (REQS, 3), 0, longest + 1)
    lengths = jnp.min(attempts, axis=1)
    chosen = jax.random.randint(second_key, (), 0, REQS)
    return jnp.where(jnp.arange(REQS, dtype=jnp.int32) == chosen, longest, lengths).astype(jnp.int32)


def shard_levels(stream_key, extent, shards, smallest, top_value):
    level, own = 1.0, jax.random.fold_in(stream_key, 6)
    for dim, parts in shards:
        heights = jnp.exp(jax.random.uniform(jax.random.fold_in(own, dim), (parts,), jnp.float32, smallest / len(shards), top_value / len(shards)))
        level = level * jnp.repeat(heights, extent[dim] // parts).reshape([-1 if axis == dim else 1 for axis in range(len(extent))])
    return level


def shared_out(own_key, own, number, rows, amount, top, limit, lean):
    order = jax.random.permutation(own_key, amount)
    heavy_load, usual = load_shares(amount, rows * top, limit, lean, True), load_shares(amount, rows * top, limit, lean, False)
    places = jnp.arange(amount)

    def named(sizes, offset_by):
        used = int((sizes > 0).sum())
        fixed = max(1, used // 4)
        moved = fixed + (places - fixed + offset_by * (used - fixed)) % max(1, amount - fixed)
        return jnp.zeros((amount,), jnp.int32).at[order[jnp.where(places < fixed, places, moved)]].set(jnp.asarray(sizes, jnp.int32))

    sizes = jnp.where(number % 4 == 0, named(heavy_load, number // 4), named(usual, number - number // 4 - 1))
    mixed = jax.random.permutation(jax.random.fold_in(own, 3), amount)
    donor, receiver = mixed[0:amount // 2 * 2:2], mixed[1:amount // 2 * 2:2]
    slack = jnp.minimum(sizes[donor] - 1, limit - sizes[receiver]) // 2
    slack = jnp.where((donor == order[0]) | (receiver == order[0]) | (sizes[receiver] == 0), 0, jnp.maximum(slack, 0))
    moved = jax.random.randint(jax.random.fold_in(own, 4), (amount // 2,), 0, 1 << 20) % (slack + 1)
    sizes = sizes.at[donor].add(-moved).at[receiver].add(moved)
    labels = jnp.searchsorted(jnp.cumsum(sizes), jnp.arange(rows * top), side="right").astype(jnp.int32)
    table = labels.reshape(top, rows).T
    table = table[jax.random.permutation(jax.random.fold_in(own, 1), rows)]
    offset_by = jax.random.randint(jax.random.fold_in(own, 2), (rows, 1), 0, top)
    return jnp.take_along_axis(table, (jnp.arange(top)[None, :] + offset_by) % top, axis=1)


def load_shares(amount, total, reach, lean, full):
    portions = [(1 << 20) // math.isqrt(grade ** lean) + 1 for grade in range(1, amount + 1)]
    largest = reach if full else min(reach, max(-(-total // amount), total * portions[0] // sum(portions)))
    least = 1 if total - largest >= amount - 1 else 0
    holding, surplus = [largest] + [least] * (amount - 1), total - largest - least * (amount - 1)
    while surplus > 0:
        free = [i for i in range(1, amount) if holding[i] < largest] or [i for i in range(1, amount) if holding[i] < reach]
        pool, budget = sum([portions[i] for i in free]), surplus
        for i in free:
            more = min(reach - holding[i], max(1, budget * portions[i] // pool), surplus)
            holding[i] = holding[i] + more
            surplus = surplus - more
    return np.array(holding)


def centred(own_key, dims, width, limit, shards=(), kind=jnp.bfloat16):
    drawn = width * jax.random.normal(own_key, dims, jnp.float32)
    if shards:
        drawn = drawn * shard_levels(own_key, dims, shards, -0.22, 0.18)
    return jnp.clip(drawn, -limit, limit).astype(kind)


def setup_inputs(seed: int = 0) -> dict:
    key_list = jax.random.split(jax.random.key(seed), 12)
    queries = draw_queries(jax.random.fold_in(key_list[11], 71), 0)
    new_kv = draw_new_kv(jax.random.fold_in(key_list[11], 71), 0)
    cache_pool = centred(key_list[2], (REQS, MAXPG, 2, PAGE, D), 1.0, 4.0, ((0, 8), (1, 4)))
    page_table = draw_page_table(jax.random.fold_in(key_list[11], 71), 0)
    cached_len = draw_cached_len(jax.random.fold_in(key_list[11], 71), 0)
    residual = centred(key_list[5], (TOKENS, D), 0.03, 0.1796875, ((0, 8),))
    norm_gain = jnp.clip(1.0 + 0.18 * jax.random.normal(key_list[6], (D,), jnp.float32), 0.1, 1.9)
    expert_ids_keys = jax.random.split(jax.random.fold_in(key_list[7], 1), TOKENS // TOKW)
    expert_ids_turns = jax.random.permutation(jax.random.fold_in(key_list[7], 3), TOKENS // TOKW)
    expert_ids = jax.vmap(lambda own, number: shared_out(jax.random.fold_in(key_list[7], 2), own, number, TOKW, E, 2, CAP, 1))(expert_ids_keys, expert_ids_turns).reshape((TOKENS, 2))
    route_weight = jnp.clip(0.1 + 0.9 * jax.random.uniform(key_list[8], (TOKENS, 2), jnp.float32) ** shard_levels(key_list[8], (TOKENS, 2), ((0, 8),), -0.2, 0.2), 0.1, 1.0)
    w_gate_up = centred(key_list[9], (E, D, 2, FF), D ** -0.5, 0.125, ((1, 4), (3, 8)))
    w_down = centred(key_list[10], (E, FF, D), FF ** -0.5, 0.078125, ((1, 8), (2, 4)))
    return {"queries": queries, "new_kv": new_kv, "cache_pool": cache_pool, "page_table": page_table, "cached_len": cached_len, "residual": residual, "norm_gain": norm_gain, "expert_ids": expert_ids, "route_weight": route_weight, "w_gate_up": w_gate_up, "w_down": w_down}


NEG_FILL = -1e+30
SCORE_SCALE = 0.125
EPSILON = 1e-05

def attend_one(inputs):
    query_rows, new_pair, page_rows, table_row, length_one = inputs
    groups = N_NARROW
    local_new = NEWTOK // groups
    ordered = jnp.take(page_rows, table_row.astype(jnp.int32), axis=0)
    cache_keys = ordered[:, 0].astype(jnp.float32).reshape(PG_DEV, groups, PAGE, HEADS, HD)
    cache_vals = ordered[:, 1].astype(jnp.float32).reshape(PG_DEV, groups, PAGE, HEADS, HD)
    new_keys = new_pair[0].astype(jnp.float32).reshape(groups, local_new, HEADS, HD)
    new_vals = new_pair[1].astype(jnp.float32).reshape(groups, local_new, HEADS, HD)
    query_heads = query_rows.astype(jnp.float32).reshape(NEWTOK, HEADS, HD)
    cache_scores = jnp.einsum('qhd,inphd->hqinp', query_heads, cache_keys) * SCORE_SCALE
    new_scores = jnp.einsum('qhd,nchd->hqnc', query_heads, new_keys) * SCORE_SCALE
    page_index = jnp.arange(PG_DEV, dtype=jnp.int32)[:, None, None] * groups + jnp.arange(groups, dtype=jnp.int32)[None, :, None]
    cache_pos = page_index * PAGE + jnp.arange(PAGE, dtype=jnp.int32)[None, None, :]
    cache_valid = cache_pos < length_one
    new_pos = jnp.arange(NEWTOK, dtype=jnp.int32).reshape(groups, local_new)
    new_valid = new_pos[None, :, :] <= jnp.arange(NEWTOK, dtype=jnp.int32)[:, None, None]
    cache_scores = jnp.where(cache_valid[None, None], cache_scores, NEG_FILL)
    new_scores = jnp.where(new_valid[None], new_scores, NEG_FILL)
    score_top = jnp.maximum(lax.optimization_barrier(jnp.max(cache_scores, axis=(2, 3, 4))), lax.optimization_barrier(jnp.max(new_scores, axis=(2, 3))))
    cache_weights = jnp.where(cache_valid[None, None], jnp.exp(cache_scores - score_top[:, :, None, None, None]), 0.0)
    new_weights = jnp.where(new_valid[None], jnp.exp(new_scores - score_top[:, :, None, None]), 0.0)
    denominator = lax.optimization_barrier(jnp.sum(cache_weights, axis=(2, 4))) + lax.optimization_barrier(jnp.sum(new_weights, axis=3))
    cache_round = lax.optimization_barrier(cache_weights.astype(jnp.bfloat16)).astype(jnp.float32)
    new_round = lax.optimization_barrier(new_weights.astype(jnp.bfloat16)).astype(jnp.float32)
    numerator = jnp.einsum('hqinp,inphd->nqhd', cache_round, cache_vals) + jnp.einsum('hqnc,nchd->nqhd', new_round, new_vals)
    numerator = lax.optimization_barrier(numerator.astype(jnp.bfloat16)).astype(jnp.float32)
    denominator = lax.optimization_barrier(denominator.astype(jnp.bfloat16)).astype(jnp.float32)
    total_num = lax.optimization_barrier(jnp.sum(numerator, axis=0))
    total_den = lax.optimization_barrier(jnp.sum(denominator, axis=2))
    return (total_num / jnp.transpose(total_den)[:, :, None]).reshape(NEWTOK, D)

def reference(queries, new_kv, cache_pool, page_table, cached_len, residual, norm_gain, expert_ids, route_weight, w_gate_up, w_down):
    attention = lax.map(attend_one, (queries, new_kv, cache_pool, page_table, cached_len))
    hidden = residual.astype(jnp.float32) + attention.reshape(TOKENS, D)
    spread = lax.optimization_barrier(jnp.mean(hidden * hidden, axis=1, keepdims=True))
    normed = (hidden * lax.rsqrt(spread + EPSILON) * norm_gain).astype(jnp.bfloat16)
    block_ids = expert_ids.reshape(N_WIDE, TOKW * 2).astype(jnp.int32)
    onehot = (block_ids[:, :, None] == jnp.arange(E, dtype=jnp.int32)[None, None, :]).astype(jnp.int32)
    earlier = jnp.cumsum(onehot, axis=1) - onehot
    position = lax.optimization_barrier(jnp.sum(earlier * onehot, axis=2)).astype(jnp.int32)
    slot_ids = (block_ids * CAP + position).astype(jnp.int32)
    source_rows = jnp.repeat(normed.reshape(N_WIDE, TOKW, D), 2, axis=1)
    block_index = jnp.arange(N_WIDE, dtype=jnp.int32)[:, None]
    dispatched = jnp.zeros((N_WIDE, E * CAP, D), jnp.bfloat16).at[block_index, slot_ids].set(source_rows)
    grouped = dispatched.reshape(N_WIDE, E, CAP, D)
    gate_table = w_gate_up.reshape(E, D, 2 * FF)
    width_part = D // N_NARROW
    gate_up = jnp.zeros((N_WIDE, E, CAP, 2 * FF), jnp.float32)
    for group_index in range(N_NARROW):
        offset = group_index * width_part
        partial_term = jnp.einsum('wecd,edf->wecf', grouped[..., offset:offset + width_part].astype(jnp.float32), gate_table[:, offset:offset + width_part].astype(jnp.float32))
        gate_up = gate_up + lax.optimization_barrier(partial_term.astype(jnp.bfloat16)).astype(jnp.float32)
    activated = (jax.nn.silu(gate_up[..., :FF]) * gate_up[..., FF:]).astype(jnp.bfloat16)
    unit_part = FF // N_WIDE
    expert_out = jnp.zeros((N_WIDE, E, CAP, D), jnp.float32)
    for group_index in range(N_WIDE):
        offset = group_index * unit_part
        partial_term = jnp.einsum('wecf,efd->wecd', activated[..., offset:offset + unit_part].astype(jnp.float32), w_down[:, offset:offset + unit_part].astype(jnp.float32))
        expert_out = expert_out + lax.optimization_barrier(partial_term.astype(jnp.bfloat16)).astype(jnp.float32)
    flat_out = expert_out.reshape(N_WIDE, E * CAP, D)
    picked = jnp.take_along_axis(flat_out, slot_ids[:, :, None], axis=1).reshape(N_WIDE, TOKW, 2, D)
    mixing = route_weight.reshape(N_WIDE, TOKW, 2)
    mixed = mixing[:, :, 0:1] * picked[:, :, 0] + mixing[:, :, 1:2] * picked[:, :, 1]
    return (hidden + mixed.reshape(TOKENS, D)).astype(jnp.bfloat16)
```

```python
import jax
import jax.numpy as jnp
from jax import lax
from jax.sharding import PartitionSpec as P

HD = 64
CAP = 80
CHUNKS = 4

NEG_FILL = -1e30
SCORE_SCALE = 0.125
EPSILON = 1e-05


def local(
    queries,
    new_kv,
    cache_pool,
    page_table,
    cached_len,
    residual,
    norm_gain,
    expert_ids,
    route_weight,
    w_gate_up,
    w_down,
):
    narrow_count = lax.axis_size("narrow")
    narrow_pos = lax.axis_index("narrow")
    wide_count = lax.axis_size("wide")
    req_here, new_len, model_width = queries.shape
    head_count = model_width // HD
    slot_count = cache_pool.shape[1]
    page_len = cache_pool.shape[3]
    local_new = new_kv.shape[2]
    table_len = page_table.shape[1]
    query_heads = queries.reshape(req_here, new_len, head_count, HD)
    cache_keys = cache_pool[:, :, 0].reshape(req_here, slot_count * page_len, head_count, HD)
    cache_vals = cache_pool[:, :, 1].reshape(req_here, slot_count * page_len, head_count, HD)
    new_keys = new_kv[:, 0].reshape(req_here, local_new, head_count, HD)
    new_vals = new_kv[:, 1].reshape(req_here, local_new, head_count, HD)
    own_slots = narrow_pos * slot_count + jnp.arange(slot_count, dtype=jnp.int32)
    matches = page_table[:, None, :] == own_slots[None, :, None]
    logical = jnp.sum(
        jnp.where(matches, jnp.arange(table_len, dtype=jnp.int32)[None, None, :], 0), axis=2
    )
    key_pos = logical[:, :, None] * page_len + jnp.arange(page_len, dtype=jnp.int32)[None, None, :]
    cache_valid = key_pos.reshape(req_here, slot_count * page_len) < cached_len[:, None]
    new_pos = narrow_pos * local_new + jnp.arange(local_new, dtype=jnp.int32)
    new_valid = new_pos[None, :] <= jnp.arange(new_len, dtype=jnp.int32)[:, None]
    cache_scores = (
        jnp.einsum("rqhd,rkhd->rhqk", query_heads, cache_keys, preferred_element_type=jnp.float32)
        * SCORE_SCALE
    )
    new_scores = (
        jnp.einsum("rqhd,rkhd->rhqk", query_heads, new_keys, preferred_element_type=jnp.float32)
        * SCORE_SCALE
    )
    cache_scores = jnp.where(cache_valid[:, None, None, :], cache_scores, NEG_FILL)
    new_scores = jnp.where(new_valid[None, None], new_scores, NEG_FILL)
    own_top = jnp.maximum(jnp.max(cache_scores, axis=3), jnp.max(new_scores, axis=3))
    cache_weights = jnp.where(
        cache_valid[:, None, None, :], jnp.exp(cache_scores - own_top[..., None]), 0.0
    )
    new_weights = jnp.where(new_valid[None, None], jnp.exp(new_scores - own_top[..., None]), 0.0)
    denominator = jnp.sum(cache_weights, axis=3) + jnp.sum(new_weights, axis=3)
    numerator = jnp.einsum(
        "rhqk,rkhd->rqhd",
        cache_weights.astype(jnp.bfloat16),
        cache_vals,
        preferred_element_type=jnp.float32,
    )
    numerator = numerator + jnp.einsum(
        "rhqk,rkhd->rqhd",
        new_weights.astype(jnp.bfloat16),
        new_vals,
        preferred_element_type=jnp.float32,
    )
    numerator = numerator.reshape(req_here * new_len, model_width).astype(jnp.bfloat16)
    stats = jnp.stack([own_top, denominator])
    stats = lax.all_gather(stats, "narrow", axis=0)
    feature_count = model_width // narrow_count
    token_rows = req_here * new_len
    pieces = numerator.reshape(token_rows, narrow_count, feature_count).transpose(1, 0, 2)
    pieces = lax.all_to_all(pieces, "narrow", 0, 0).astype(jnp.float32)
    tops, dens = stats[:, 0], stats[:, 1]
    factor = jnp.exp(tops - jnp.max(tops, axis=0, keepdims=True))
    factor = factor / jnp.sum(factor * dens, axis=0, keepdims=True)
    factor = factor.transpose(0, 1, 3, 2).reshape(narrow_count * token_rows, head_count)
    column_head = (narrow_pos * feature_count + jnp.arange(feature_count, dtype=jnp.int32)) // HD
    spread_heads = (
        jnp.arange(head_count, dtype=jnp.int32)[:, None] == column_head[None, :]
    ).astype(jnp.float32)
    factor = jnp.dot(factor, spread_heads, precision=lax.Precision.HIGHEST)
    attention = jnp.sum(pieces * factor.reshape(pieces.shape), axis=0)
    residual_share = lax.dynamic_slice_in_dim(residual, narrow_pos * feature_count, feature_count, 1)
    gain_share = lax.dynamic_slice_in_dim(norm_gain, narrow_pos * feature_count, feature_count, 0)
    hidden = residual_share.astype(jnp.float32) + attention
    squares = lax.all_gather(jnp.sum(hidden * hidden, axis=1), ("wide", "narrow"), axis=0)
    all_rows = lax.all_gather((hidden * gain_share).astype(jnp.bfloat16), "wide", axis=0)
    squares = jnp.sum(squares.reshape(wide_count, narrow_count, token_rows), axis=1)
    scale = lax.rsqrt(squares / model_width + EPSILON)
    normed = (all_rows.astype(jnp.float32) * scale[:, :, None]).astype(jnp.bfloat16)

    all_ids = lax.all_gather(expert_ids, "wide", axis=0)
    all_route = lax.all_gather(route_weight, "wide", axis=0)
    chips = narrow_count // 2
    chip, core = narrow_pos // 2, narrow_pos % 2
    block = wide_count // narrow_count
    far = jnp.arange(narrow_count, dtype=jnp.int32)
    owner = ((chip + far % chips) % chips) * 2 + (core + far // chips) % 2
    order = (owner[:, None] * block + jnp.arange(block, dtype=jnp.int32)[None, :]).reshape(-1)
    normed = normed[order]
    all_ids = all_ids[order]
    all_route = all_route[order]
    assign_count = token_rows * 2
    expert_count = w_gate_up.shape[0]
    flat_ids = all_ids.reshape(wide_count, assign_count)
    onehot = (
        flat_ids[:, :, None] == jnp.arange(expert_count, dtype=jnp.int32)[None, None, :]
    ).astype(jnp.bfloat16)
    strict_lower = (jnp.arange(assign_count)[:, None] > jnp.arange(assign_count)[None, :]).astype(
        jnp.bfloat16
    )
    earlier = jnp.einsum("ab,wbe->wae", strict_lower, onehot, preferred_element_type=jnp.float32)
    position = jnp.sum(earlier * onehot, axis=2).astype(jnp.int32)
    slot_pairs = (flat_ids * CAP + position).reshape(wide_count, token_rows, 2)
    slot_range = jnp.arange(expert_count * CAP, dtype=jnp.int32)
    picks = slot_range[None, :, None, None] == slot_pairs[:, None, :, :]
    dispatch = jnp.any(picks, axis=3).astype(jnp.bfloat16)
    combine_table = jnp.sum(jnp.where(picks, all_route[:, None, :, :], 0.0), axis=3)
    combine_table = combine_table.astype(jnp.bfloat16).reshape(
        wide_count, expert_count, CAP, token_rows
    )
    dispatch = dispatch.reshape(wide_count, expert_count, CAP, token_rows)
    placed = jnp.einsum(
        "wect,wtd->ewcd", dispatch, normed, preferred_element_type=jnp.float32
    ).astype(jnp.bfloat16)
    placed = placed.reshape(expert_count, wide_count * CAP, feature_count)

    core_pairs = [(n, n ^ 1) for n in range(narrow_count)]

    def chip_pairs(step):
        return [(n, (n + 2 * step) % narrow_count) for n in range(narrow_count)]

    table = jnp.transpose(w_gate_up, (2, 0, 1, 3))
    per_chunk = expert_count // CHUNKS
    rows_half = wide_count * CAP // 2
    rows_own = rows_half // chips
    out_chunks = []
    for chunk in range(CHUNKS):
        picked = slice(chunk * per_chunk, (chunk + 1) * per_chunk)
        partial = jnp.einsum(
            "erd,gedf->gerf", placed[picked], table[:, picked], preferred_element_type=jnp.float32
        ).astype(jnp.bfloat16)
        near = lax.ppermute(partial[:, :, rows_half:], "narrow", core_pairs)
        both = (
            partial[:, :, :rows_half].astype(jnp.float32) + near.astype(jnp.float32)
        )
        own = both[:, :, :rows_own]
        sent = both[:, :, rows_own:].astype(jnp.bfloat16)
        for step in range(1, chips):
            arrived = lax.ppermute(
                sent[:, :, (step - 1) * rows_own : step * rows_own], "narrow", chip_pairs(step)
            )
            own = own + arrived.astype(jnp.float32)
        active = (jax.nn.silu(own[0]) * own[1]).astype(jnp.bfloat16)
        mine = [active] + [
            lax.ppermute(active, "narrow", chip_pairs(chips - step)) for step in range(1, chips)
        ]
        mine = jnp.concatenate(mine, axis=1)
        other = lax.ppermute(mine, "narrow", core_pairs)
        whole = jnp.concatenate([mine, other], axis=1)
        out_chunks.append(
            jnp.einsum(
                "erf,efd->erd", whole, w_down[picked], preferred_element_type=jnp.float32
            ).astype(jnp.bfloat16)
        )
    outs = jnp.concatenate(out_chunks, axis=0).reshape(
        expert_count, wide_count, CAP, feature_count
    )
    mixed = jnp.einsum(
        "wect,ewcd->wtd", combine_table, outs, preferred_element_type=jnp.float32
    ).astype(jnp.bfloat16)
    back = jnp.argsort(order)
    mixed = lax.all_to_all(mixed[back], "wide", 0, 0)
    mixed = jnp.sum(mixed.astype(jnp.float32), axis=0)
    return (hidden + mixed).astype(jnp.bfloat16)


def solution(mesh):
    return jax.shard_map(
        local,
        mesh=mesh,
        in_specs=(
            P("wide", None, None),
            P("wide", None, "narrow", None),
            P("wide", "narrow", None, None, None),
            P("wide", None),
            P("wide"),
            P("wide", None),
            P(),
            P("wide", None),
            P("wide", None),
            P(None, "narrow", None, "wide"),
            P(None, "wide", "narrow"),
        ),
        out_specs=P("wide", "narrow"),
        check_vma=False,
    )
```

```python
import jax
import jax.numpy as jnp
from jax import lax
from jax.experimental import pallas as pl
from jax.experimental.pallas import tpu as pltpu
from jax.sharding import PartitionSpec as P

HD = 64
CAP = 80
CHUNKS = 4
GROUP = 384
PAIR = 2 * HD

NEG_FILL = -1e30
SCORE_SCALE = 0.125
EPSILON = 1e-05


def attend_kernel(valid_ref, causal_ref, query_ref, cache_ref, new_ref, numer_ref, stats_ref):
    slots, page = cache_ref.shape[1], cache_ref.shape[3]
    heads = GROUP // HD
    rows = query_ref.shape[1]
    valid = valid_ref[0] > 0
    causal = causal_ref[...] > 0
    lower = lax.broadcasted_iota(jnp.int32, (rows, PAIR), 1) < HD
    nt = (((1,), (1,)), ((), ()))
    for pair in range(GROUP // PAIR):
        cols = slice(pair * PAIR, (pair + 1) * PAIR)
        query = query_ref[0, :, cols]
        keys = cache_ref[0, :, 0, :, cols].reshape(slots * page, PAIR)
        vals = cache_ref[0, :, 1, :, cols].reshape(slots * page, PAIR)
        new_keys = new_ref[0, 0, :, cols]
        new_vals = new_ref[0, 1, :, cols]
        sums = []
        for side in range(2):
            own = jnp.where(lower if side == 0 else ~lower, query, jnp.zeros_like(query))
            far = lax.dot_general(own, keys, nt, preferred_element_type=jnp.float32)
            near = lax.dot_general(own, new_keys, nt, preferred_element_type=jnp.float32)
            far = jnp.where(valid, far * SCORE_SCALE, NEG_FILL)
            near = jnp.where(causal, near * SCORE_SCALE, NEG_FILL)
            top = jnp.maximum(
                jnp.max(far, axis=1, keepdims=True), jnp.max(near, axis=1, keepdims=True)
            )
            far = jnp.where(valid, jnp.exp(far - top), 0.0)
            near = jnp.where(causal, jnp.exp(near - top), 0.0)
            total = jnp.sum(far, axis=1, keepdims=True) + jnp.sum(near, axis=1, keepdims=True)
            sums.append(
                jnp.dot(far.astype(jnp.bfloat16), vals, preferred_element_type=jnp.float32)
                + jnp.dot(near.astype(jnp.bfloat16), new_vals, preferred_element_type=jnp.float32)
            )
            head = 2 * pair + side
            stats_ref[0, 0, :, head : head + 1] = top
            stats_ref[0, 0, :, heads + head : heads + head + 1] = total
        numer_ref[0, :, cols] = jnp.where(lower, sums[0], sums[1]).astype(jnp.bfloat16)


def attend(queries, new_kv, cache_pool, cache_valid, new_valid):
    reqs, rows, width = queries.shape
    slots, page = cache_pool.shape[1], cache_pool.shape[3]
    new_rows = new_kv.shape[2]
    groups = width // GROUP
    heads = GROUP // HD
    numer, stats = pl.pallas_call(
        attend_kernel,
        grid=(reqs, groups),
        in_specs=[
            pl.BlockSpec((1, 1, slots * page), lambda r, g: (r, 0, 0)),
            pl.BlockSpec((rows, new_rows), lambda r, g: (0, 0)),
            pl.BlockSpec((1, rows, GROUP), lambda r, g: (r, 0, g)),
            pl.BlockSpec((1, slots, 2, page, GROUP), lambda r, g: (r, 0, 0, 0, g)),
            pl.BlockSpec((1, 2, new_rows, GROUP), lambda r, g: (r, 0, 0, g)),
        ],
        out_specs=[
            pl.BlockSpec((1, rows, GROUP), lambda r, g: (r, 0, g)),
            pl.BlockSpec((1, 1, rows, 2 * heads), lambda r, g: (r, g, 0, 0)),
        ],
        out_shape=[
            jax.ShapeDtypeStruct((reqs, rows, width), jnp.bfloat16),
            jax.ShapeDtypeStruct((reqs, groups, rows, 2 * heads), jnp.float32),
        ],
        compiler_params=pltpu.CompilerParams(vmem_limit_bytes=32 * 2**20),
    )(
        cache_valid.astype(jnp.float32)[:, None, :],
        new_valid.astype(jnp.float32),
        queries,
        cache_pool,
        new_kv,
    )
    stats = stats.reshape(reqs, groups, rows, 2, heads).transpose(3, 0, 1, 4, 2)
    return numer, stats.reshape(2, reqs, groups * heads, rows)


def local(
    queries,
    new_kv,
    cache_pool,
    page_table,
    cached_len,
    residual,
    norm_gain,
    expert_ids,
    route_weight,
    w_gate_up,
    w_down,
):
    narrow_count = lax.axis_size("narrow")
    narrow_pos = lax.axis_index("narrow")
    wide_count = lax.axis_size("wide")
    req_here, new_len, model_width = queries.shape
    head_count = model_width // HD
    slot_count = cache_pool.shape[1]
    page_len = cache_pool.shape[3]
    local_new = new_kv.shape[2]
    table_len = page_table.shape[1]
    own_slots = narrow_pos * slot_count + jnp.arange(slot_count, dtype=jnp.int32)
    matches = page_table[:, None, :] == own_slots[None, :, None]
    logical = jnp.sum(
        jnp.where(matches, jnp.arange(table_len, dtype=jnp.int32)[None, None, :], 0), axis=2
    )
    key_pos = logical[:, :, None] * page_len + jnp.arange(page_len, dtype=jnp.int32)[None, None, :]
    cache_valid = key_pos.reshape(req_here, slot_count * page_len) < cached_len[:, None]
    new_pos = narrow_pos * local_new + jnp.arange(local_new, dtype=jnp.int32)
    new_valid = new_pos[None, :] <= jnp.arange(new_len, dtype=jnp.int32)[:, None]
    numerator, stats = attend(
        queries,
        new_kv,
        cache_pool,
        cache_valid.reshape(req_here, slot_count * page_len),
        new_valid,
    )
    stats = lax.all_gather(stats, "narrow", axis=0)
    feature_count = model_width // narrow_count
    token_rows = req_here * new_len
    pieces = numerator.reshape(token_rows, narrow_count, feature_count).transpose(1, 0, 2)
    pieces = lax.all_to_all(pieces, "narrow", 0, 0).astype(jnp.float32)
    tops, dens = stats[:, 0], stats[:, 1]
    factor = jnp.exp(tops - jnp.max(tops, axis=0, keepdims=True))
    factor = factor / jnp.sum(factor * dens, axis=0, keepdims=True)
    factor = factor.transpose(0, 1, 3, 2).reshape(narrow_count * token_rows, head_count)
    column_head = (narrow_pos * feature_count + jnp.arange(feature_count, dtype=jnp.int32)) // HD
    spread_heads = (
        jnp.arange(head_count, dtype=jnp.int32)[:, None] == column_head[None, :]
    ).astype(jnp.float32)
    factor = jnp.dot(factor, spread_heads, precision=lax.Precision.HIGHEST)
    attention = jnp.sum(pieces * factor.reshape(pieces.shape), axis=0)
    residual_share = lax.dynamic_slice_in_dim(residual, narrow_pos * feature_count, feature_count, 1)
    gain_share = lax.dynamic_slice_in_dim(norm_gain, narrow_pos * feature_count, feature_count, 0)
    hidden = residual_share.astype(jnp.float32) + attention
    squares = lax.all_gather(jnp.sum(hidden * hidden, axis=1), ("wide", "narrow"), axis=0)
    all_rows = lax.all_gather((hidden * gain_share).astype(jnp.bfloat16), "wide", axis=0)
    squares = jnp.sum(squares.reshape(wide_count, narrow_count, token_rows), axis=1)
    scale = lax.rsqrt(squares / model_width + EPSILON)
    normed = (all_rows.astype(jnp.float32) * scale[:, :, None]).astype(jnp.bfloat16)

    routing = jnp.concatenate(
        [expert_ids.astype(jnp.float32).reshape(-1), route_weight.reshape(-1)]
    )
    routing = lax.all_gather(routing, "wide", axis=0).reshape(wide_count, 2, token_rows, 2)
    all_ids = routing[:, 0].astype(jnp.int32)
    all_route = routing[:, 1]
    chips = narrow_count // 2
    chip, core = narrow_pos // 2, narrow_pos % 2
    block = wide_count // narrow_count
    far = jnp.arange(narrow_count, dtype=jnp.int32)
    owner = ((chip + far % chips) % chips) * 2 + (core + far // chips) % 2
    order = (owner[:, None] * block + jnp.arange(block, dtype=jnp.int32)[None, :]).reshape(-1)
    normed = normed[order]
    all_ids = all_ids[order]
    all_route = all_route[order]
    assign_count = token_rows * 2
    expert_count = w_gate_up.shape[0]
    flat_ids = all_ids.reshape(wide_count, assign_count)
    onehot = (
        flat_ids[:, :, None] == jnp.arange(expert_count, dtype=jnp.int32)[None, None, :]
    ).astype(jnp.bfloat16)
    strict_lower = (jnp.arange(assign_count)[:, None] > jnp.arange(assign_count)[None, :]).astype(
        jnp.bfloat16
    )
    earlier = jnp.einsum("ab,wbe->wae", strict_lower, onehot, preferred_element_type=jnp.float32)
    position = jnp.sum(earlier * onehot, axis=2).astype(jnp.int32)
    slot_pairs = (flat_ids * CAP + position).reshape(wide_count, token_rows, 2)
    slot_range = jnp.arange(expert_count * CAP, dtype=jnp.int32)
    picks = slot_range[None, :, None, None] == slot_pairs[:, None, :, :]
    dispatch = jnp.any(picks, axis=3).astype(jnp.bfloat16)
    combine_table = jnp.sum(jnp.where(picks, all_route[:, None, :, :], 0.0), axis=3)
    combine_table = combine_table.astype(jnp.bfloat16).reshape(
        wide_count, expert_count, CAP, token_rows
    )
    dispatch = dispatch.reshape(wide_count, expert_count, CAP, token_rows)
    placed = jnp.einsum(
        "wect,wtd->ewcd", dispatch, normed, preferred_element_type=jnp.float32
    ).astype(jnp.bfloat16)
    placed = placed.reshape(expert_count, wide_count * CAP, feature_count)

    core_pairs = [(n, n ^ 1) for n in range(narrow_count)]

    def chip_pairs(step):
        return [(n, (n + 2 * step) % narrow_count) for n in range(narrow_count)]

    table = jnp.transpose(w_gate_up, (2, 0, 1, 3))
    per_chunk = expert_count // CHUNKS
    rows_half = wide_count * CAP // 2
    rows_own = rows_half // chips
    out_chunks = []
    sents, owns = [], []
    for chunk in range(CHUNKS):
        picked = slice(chunk * per_chunk, (chunk + 1) * per_chunk)
        rows_in = placed[picked]
        if chunk >= 2:
            rows_in, sents[chunk - 2] = lax.optimization_barrier((rows_in, sents[chunk - 2]))
        partial = jnp.einsum(
            "erd,gedf->gerf", rows_in, table[:, picked], preferred_element_type=jnp.float32
        ).astype(jnp.bfloat16)
        near = lax.ppermute(partial[:, :, rows_half:], "narrow", core_pairs)
        both = (
            partial[:, :, :rows_half].astype(jnp.float32) + near.astype(jnp.float32)
        )
        owns.append(both[:, :, :rows_own])
        sents.append(both[:, :, rows_own:].astype(jnp.bfloat16))
    for chunk in range(CHUNKS):
        picked = slice(chunk * per_chunk, (chunk + 1) * per_chunk)
        own, sent = owns[chunk], sents[chunk]
        for step in range(1, chips):
            arrived = lax.ppermute(
                sent[:, :, (step - 1) * rows_own : step * rows_own], "narrow", chip_pairs(step)
            )
            own = own + arrived.astype(jnp.float32)
        active = (jax.nn.silu(own[0]) * own[1]).astype(jnp.bfloat16)
        mine = [active] + [
            lax.ppermute(active, "narrow", chip_pairs(chips - step)) for step in range(1, chips)
        ]
        mine = jnp.concatenate(mine, axis=1)
        other = lax.ppermute(mine, "narrow", core_pairs)
        if out_chunks:
            other, out_chunks[-1] = lax.optimization_barrier((other, out_chunks[-1]))
        whole = jnp.concatenate([mine, other], axis=1)
        out_chunks.append(
            jnp.einsum(
                "erf,efd->erd", whole, w_down[picked], preferred_element_type=jnp.float32
            ).astype(jnp.bfloat16)
        )
    outs = jnp.concatenate(out_chunks, axis=0).reshape(
        expert_count, wide_count, CAP, feature_count
    )
    mixed = jnp.einsum(
        "wect,ewcd->wtd", combine_table, outs, preferred_element_type=jnp.float32
    ).astype(jnp.bfloat16)
    back = jnp.argsort(order)
    mixed = lax.all_to_all(mixed[back], "wide", 0, 0)
    mixed = jnp.sum(mixed.astype(jnp.float32), axis=0)
    return (hidden + mixed).astype(jnp.bfloat16)


def solution(mesh):
    return jax.shard_map(
        local,
        mesh=mesh,
        in_specs=(
            P("wide", None, None),
            P("wide", None, "narrow", None),
            P("wide", "narrow", None, None, None),
            P("wide", None),
            P("wide"),
            P("wide", None),
            P(),
            P("wide", None),
            P("wide", None),
            P(None, "narrow", None, "wide"),
            P(None, "wide", "narrow"),
        ),
        out_specs=P("wide", "narrow"),
        check_vma=False,
    )
```

```python
import jax
import jax.numpy as jnp
from jax import lax
from jax.experimental import pallas as pl
from jax.experimental.pallas import tpu as pltpu
from jax.sharding import PartitionSpec as P

HD = 64
CAP = 80
CHUNKS = 4
GROUP = 384
PAIR = 2 * HD

NEG_FILL = -1e30
SCORE_SCALE = 0.125
EPSILON = 1e-05


def attend_kernel(valid_ref, causal_ref, query_ref, cache_ref, new_ref, numer_ref, stats_ref):
    slots, page = cache_ref.shape[1], cache_ref.shape[3]
    heads = GROUP // HD
    rows = query_ref.shape[1]
    valid = valid_ref[0] > 0
    causal = causal_ref[...] > 0
    lower = lax.broadcasted_iota(jnp.int32, (rows, PAIR), 1) < HD
    nt = (((1,), (1,)), ((), ()))
    for pair in range(GROUP // PAIR):
        cols = slice(pair * PAIR, (pair + 1) * PAIR)
        query = query_ref[0, :, cols]
        keys = cache_ref[0, :, 0, :, cols].reshape(slots * page, PAIR)
        vals = cache_ref[0, :, 1, :, cols].reshape(slots * page, PAIR)
        new_keys = new_ref[0, 0, :, cols]
        new_vals = new_ref[0, 1, :, cols]
        sums = []
        for side in range(2):
            own = jnp.where(lower if side == 0 else ~lower, query, jnp.zeros_like(query))
            far = lax.dot_general(own, keys, nt, preferred_element_type=jnp.float32)
            near = lax.dot_general(own, new_keys, nt, preferred_element_type=jnp.float32)
            far = jnp.where(valid, far * SCORE_SCALE, NEG_FILL)
            near = jnp.where(causal, near * SCORE_SCALE, NEG_FILL)
            top = jnp.maximum(
                jnp.max(far, axis=1, keepdims=True), jnp.max(near, axis=1, keepdims=True)
            )
            far = jnp.where(valid, jnp.exp(far - top), 0.0)
            near = jnp.where(causal, jnp.exp(near - top), 0.0)
            total = jnp.sum(far, axis=1, keepdims=True) + jnp.sum(near, axis=1, keepdims=True)
            sums.append(
                jnp.dot(far.astype(jnp.bfloat16), vals, preferred_element_type=jnp.float32)
                + jnp.dot(near.astype(jnp.bfloat16), new_vals, preferred_element_type=jnp.float32)
            )
            head = 2 * pair + side
            stats_ref[0, 0, :, head : head + 1] = top
            stats_ref[0, 0, :, heads + head : heads + head + 1] = total
        numer_ref[0, :, cols] = jnp.where(lower, sums[0], sums[1]).astype(jnp.bfloat16)


def attend(queries, new_kv, cache_pool, cache_valid, new_valid):
    reqs, rows, width = queries.shape
    slots, page = cache_pool.shape[1], cache_pool.shape[3]
    new_rows = new_kv.shape[2]
    groups = width // GROUP
    heads = GROUP // HD
    numer, stats = pl.pallas_call(
        attend_kernel,
        grid=(reqs, groups),
        in_specs=[
            pl.BlockSpec((1, 1, slots * page), lambda r, g: (r, 0, 0)),
            pl.BlockSpec((rows, new_rows), lambda r, g: (0, 0)),
            pl.BlockSpec((1, rows, GROUP), lambda r, g: (r, 0, g)),
            pl.BlockSpec((1, slots, 2, page, GROUP), lambda r, g: (r, 0, 0, 0, g)),
            pl.BlockSpec((1, 2, new_rows, GROUP), lambda r, g: (r, 0, 0, g)),
        ],
        out_specs=[
            pl.BlockSpec((1, rows, GROUP), lambda r, g: (r, 0, g)),
            pl.BlockSpec((1, 1, rows, 2 * heads), lambda r, g: (r, g, 0, 0)),
        ],
        out_shape=[
            jax.ShapeDtypeStruct((reqs, rows, width), jnp.bfloat16),
            jax.ShapeDtypeStruct((reqs, groups, rows, 2 * heads), jnp.float32),
        ],
        compiler_params=pltpu.CompilerParams(vmem_limit_bytes=32 * 2**20),
    )(
        cache_valid.astype(jnp.float32)[:, None, :],
        new_valid.astype(jnp.float32),
        queries,
        cache_pool,
        new_kv,
    )
    stats = stats.reshape(reqs, groups, rows, 2, heads).transpose(3, 0, 1, 4, 2)
    return numer, stats.reshape(2, reqs, groups * heads, rows)


def local(
    queries,
    new_kv,
    cache_pool,
    page_table,
    cached_len,
    residual,
    norm_gain,
    expert_ids,
    route_weight,
    w_gate_up,
    w_down,
):
    narrow_count = lax.axis_size("narrow")
    narrow_pos = lax.axis_index("narrow")
    wide_count = lax.axis_size("wide")
    req_here, new_len, model_width = queries.shape
    head_count = model_width // HD
    slot_count = cache_pool.shape[1]
    page_len = cache_pool.shape[3]
    local_new = new_kv.shape[2]
    table_len = page_table.shape[1]
    own_slots = narrow_pos * slot_count + jnp.arange(slot_count, dtype=jnp.int32)
    matches = page_table[:, None, :] == own_slots[None, :, None]
    logical = jnp.sum(
        jnp.where(matches, jnp.arange(table_len, dtype=jnp.int32)[None, None, :], 0), axis=2
    )
    key_pos = logical[:, :, None] * page_len + jnp.arange(page_len, dtype=jnp.int32)[None, None, :]
    cache_valid = key_pos.reshape(req_here, slot_count * page_len) < cached_len[:, None]
    new_pos = narrow_pos * local_new + jnp.arange(local_new, dtype=jnp.int32)
    new_valid = new_pos[None, :] <= jnp.arange(new_len, dtype=jnp.int32)[:, None]
    numerator, stats = attend(
        queries,
        new_kv,
        cache_pool,
        cache_valid.reshape(req_here, slot_count * page_len),
        new_valid,
    )
    stats = lax.all_gather(stats, "narrow", axis=0)
    feature_count = model_width // narrow_count
    token_rows = req_here * new_len
    pieces = numerator.reshape(token_rows, narrow_count, feature_count).transpose(1, 0, 2)
    pieces = lax.all_to_all(pieces, "narrow", 0, 0).astype(jnp.float32)
    tops, dens = stats[:, 0], stats[:, 1]
    factor = jnp.exp(tops - jnp.max(tops, axis=0, keepdims=True))
    factor = factor / jnp.sum(factor * dens, axis=0, keepdims=True)
    factor = factor.transpose(0, 1, 3, 2).reshape(narrow_count * token_rows, head_count)
    column_head = (narrow_pos * feature_count + jnp.arange(feature_count, dtype=jnp.int32)) // HD
    spread_heads = (
        jnp.arange(head_count, dtype=jnp.int32)[:, None] == column_head[None, :]
    ).astype(jnp.float32)
    factor = jnp.dot(factor, spread_heads, precision=lax.Precision.HIGHEST)
    attention = jnp.sum(pieces * factor.reshape(pieces.shape), axis=0)
    residual_share = lax.dynamic_slice_in_dim(residual, narrow_pos * feature_count, feature_count, 1)
    gain_share = lax.dynamic_slice_in_dim(norm_gain, narrow_pos * feature_count, feature_count, 0)
    hidden = residual_share.astype(jnp.float32) + attention
    squares = lax.all_gather(jnp.sum(hidden * hidden, axis=1), ("wide", "narrow"), axis=0)
    all_rows = lax.all_gather((hidden * gain_share).astype(jnp.bfloat16), "wide", axis=0)
    squares = jnp.sum(squares.reshape(wide_count, narrow_count, token_rows), axis=1)
    scale = lax.rsqrt(squares / model_width + EPSILON)
    normed = (all_rows.astype(jnp.float32) * scale[:, :, None]).astype(jnp.bfloat16)

    routing = jnp.concatenate(
        [expert_ids.astype(jnp.float32).reshape(-1), route_weight.reshape(-1)]
    )
    routing = lax.all_gather(routing, "wide", axis=0).reshape(wide_count, 2, token_rows, 2)
    all_ids = routing[:, 0].astype(jnp.int32)
    all_route = routing[:, 1]
    chips = narrow_count // 2
    chip, core = narrow_pos // 2, narrow_pos % 2
    block = wide_count // narrow_count
    far = jnp.arange(narrow_count, dtype=jnp.int32)
    owner = ((chip + far % chips) % chips) * 2 + (core + far // chips) % 2
    order = (owner[:, None] * block + jnp.arange(block, dtype=jnp.int32)[None, :]).reshape(-1)
    normed = normed[order]
    all_ids = all_ids[order]
    all_route = all_route[order]
    assign_count = token_rows * 2
    expert_count = w_gate_up.shape[0]
    flat_ids = all_ids.reshape(wide_count, assign_count)
    onehot = (
        flat_ids[:, :, None] == jnp.arange(expert_count, dtype=jnp.int32)[None, None, :]
    ).astype(jnp.bfloat16)
    strict_lower = (jnp.arange(assign_count)[:, None] > jnp.arange(assign_count)[None, :]).astype(
        jnp.bfloat16
    )
    earlier = jnp.einsum("ab,wbe->wae", strict_lower, onehot, preferred_element_type=jnp.float32)
    position = jnp.sum(earlier * onehot, axis=2).astype(jnp.int32)
    slot_pairs = (flat_ids * CAP + position).reshape(wide_count, token_rows, 2)
    slot_range = jnp.arange(expert_count * CAP, dtype=jnp.int32)
    picks = slot_range[None, :, None, None] == slot_pairs[:, None, :, :]
    dispatch = jnp.any(picks, axis=3).astype(jnp.bfloat16)
    combine_table = jnp.sum(jnp.where(picks, all_route[:, None, :, :], 0.0), axis=3)
    combine_table = combine_table.astype(jnp.bfloat16).reshape(
        wide_count, expert_count, CAP, token_rows
    )
    dispatch = dispatch.reshape(wide_count, expert_count, CAP, token_rows)
    placed = jnp.einsum(
        "wect,wtd->ewcd", dispatch, normed, preferred_element_type=jnp.float32
    ).astype(jnp.bfloat16)
    placed = placed.reshape(expert_count, wide_count * CAP, feature_count)

    core_pairs = [(n, n ^ 1) for n in range(narrow_count)]

    def chip_pairs(step):
        return [(n, (n + 2 * step) % narrow_count) for n in range(narrow_count)]

    table = jnp.transpose(w_gate_up, (2, 0, 1, 3))
    per_chunk = expert_count // CHUNKS
    rows_half = wide_count * CAP // 2
    rows_own = rows_half // chips
    total = None
    sents, owns = [], []
    for chunk in range(CHUNKS):
        picked = slice(chunk * per_chunk, (chunk + 1) * per_chunk)
        rows_in = placed[picked]
        if chunk >= 2:
            rows_in, sents[chunk - 2] = lax.optimization_barrier((rows_in, sents[chunk - 2]))
        partial = jnp.einsum(
            "erd,gedf->gerf", rows_in, table[:, picked], preferred_element_type=jnp.float32
        ).astype(jnp.bfloat16)
        near = lax.ppermute(partial[:, :, rows_half:], "narrow", core_pairs)
        both = (
            partial[:, :, :rows_half].astype(jnp.float32) + near.astype(jnp.float32)
        )
        owns.append(both[:, :, :rows_own])
        sents.append(both[:, :, rows_own:].astype(jnp.bfloat16))
    for chunk in range(CHUNKS):
        picked = slice(chunk * per_chunk, (chunk + 1) * per_chunk)
        own, sent = owns[chunk], sents[chunk]
        for step in range(1, chips):
            arrived = lax.ppermute(
                sent[:, :, (step - 1) * rows_own : step * rows_own], "narrow", chip_pairs(step)
            )
            own = own + arrived.astype(jnp.float32)
        active = (jax.nn.silu(own[0]) * own[1]).astype(jnp.bfloat16)
        mine = [active] + [
            lax.ppermute(active, "narrow", chip_pairs(chips - step)) for step in range(1, chips)
        ]
        mine = jnp.concatenate(mine, axis=1)
        other = lax.ppermute(mine, "narrow", core_pairs)
        if total is not None:
            other, total = lax.optimization_barrier((other, total))
        whole = jnp.concatenate([mine, other], axis=1)
        outs = jnp.einsum(
            "erf,efd->erd", whole, w_down[picked], preferred_element_type=jnp.float32
        ).astype(jnp.bfloat16)
        mixed = jnp.einsum(
            "wect,ewcd->wtd",
            combine_table[:, picked],
            outs.reshape(per_chunk, wide_count, CAP, feature_count),
            preferred_element_type=jnp.float32,
        )
        total = mixed if total is None else total + mixed
    mixed = total.astype(jnp.bfloat16)
    back = jnp.argsort(order)
    mixed = lax.all_to_all(mixed[back], "wide", 0, 0)
    mixed = jnp.sum(mixed.astype(jnp.float32), axis=0)
    return (hidden + mixed).astype(jnp.bfloat16)


def solution(mesh):
    return jax.shard_map(
        local,
        mesh=mesh,
        in_specs=(
            P("wide", None, None),
            P("wide", None, "narrow", None),
            P("wide", "narrow", None, None, None),
            P("wide", None),
            P("wide"),
            P("wide", None),
            P(),
            P("wide", None),
            P("wide", None),
            P(None, "narrow", None, "wide"),
            P(None, "wide", "narrow"),
        ),
        out_specs=P("wide", "narrow"),
        check_vma=False,
    )
```
